128 devices in a mesh: ctx: 16 (over z_lo, x, core), wide: 8 (over z_hi, y).
Axes of the slice: x: 4, y: 4, z: 4 (z_hi: 2, z_lo: 2; z = z_hi * 2 + z_lo), core: 2. Of those that a mesh axis runs over, the one named last changes fastest.
Arguments:
- queries: bfloat16 [2048, 4, 4096], P('ctx', None, 'wide'), may hold values from -80 to 80
- new_entries: bfloat16 [2048, 4, 1024], P('ctx', None, 'wide'), may hold values from -8 to 8
- cached_entries: bfloat16 [8192, 4, 1024], P('ctx', None, 'wide'), may hold values from -12 to 12
- cache_lengths: int32 [4], replicated, may hold values from 1024 to 8192, as said below
- residual: bfloat16 [2048, 4, 2880], P(('ctx', 'wide')), may hold values from -6 to 6
- out_weight: bfloat16 [4096, 2880], P('wide', 'ctx'), may hold values from -0.09375 to 0.09375
- norm_gain: float32 [2880], replicated, may hold values from 0.1 to 1.9
- route_experts: int32 [2048, 4, 4], P(('ctx', 'wide')), may hold values from 0 to 127, all different within a row; in each aligned block of 64 rows (0 to 63, 64 to 127, ..., all dimensions but the last counted through in order) at most 4 rows name the same one
- route_weights: float32 [2048, 4, 4], P(('ctx', 'wide')), may hold values from 0.1 to 0.6
- inner_weight: bfloat16 [128, 2880, 2880], P(('ctx', 'wide')), may hold values from -0.109375 to 0.109375
- outer_weight: bfloat16 [128, 1440, 2880], P(('ctx', 'wide')), may hold values from -0.15625 to 0.15625
Outputs:
- layer_out: bfloat16 [2048, 4, 2880], P(('ctx', 'wide'))
The draws below stay inside these ranges and needn't reach their ends.
Inputs may be any that keep to these rules, and one draw needn't show every extreme that they name: The cached positions of prompt p in use are 0 to cache_lengths[p] - 1, and the stretch follows them; some prompt uses all 8192 positions. `route_experts`: each token names 4 different experts; among the 64 tokens of one device (aligned blocks of rows in stretch then prompt order) no expert is named more than 4 times, and that many in some block.
All inputs are finite; a program needn't handle non-finite values.
Results may differ from the reference program's by a relative error of at most 0.018.
Values may be sent and summed in bfloat16 or wider, within the bound.
No kernel may reach another device: no remote copies, remote signals or barrier semaphores. Data moves between devices by JAX's collectives and lax.ppermute only.
A program may use at most 384 MiB of HBM per device.

```python
import math
import jax
import jax.numpy as jnp
import numpy as np
from jax import lax

D = 2880
Q_HEADS = 64
KV_HEADS = 8
HEAD_DIM = 64
FFW = 1440
TOP = 4
PROMPTS = 4
TOK_DEV = 64
EXPERTS = 128
STRETCH = 2048
CACHE = 8192
CAP = 4


def draw_queries(key, part):
    key = jax.random.fold_in(key, 11)
    values = jnp.clip(jax.random.normal(key, (STRETCH, PROMPTS, Q_HEADS * HEAD_DIM), jnp.float32) * 1.7, -8.0, 8.0)
    return values.astype(jnp.bfloat16)


def draw_cached_entries(key, part):
    key = jax.random.fold_in(key, 23)
    values = jnp.clip(jax.random.normal(key, (CACHE, PROMPTS, KV_HEADS, 2, HEAD_DIM), jnp.float32) * 1.5, -8.0, 8.0)
    return values.reshape(CACHE, PROMPTS, KV_HEADS * 2 * HEAD_DIM).astype(jnp.bfloat16)


def draw_cache_lengths(key, part):
    key = jax.random.fold_in(key, 5)
    first, second = jax.random.split(key)
    drawn = jax.random.randint(first, (PROMPTS,), CACHE // 8, CACHE + 1)
    full = jax.random.randint(second, (), 0, PROMPTS)
    return jnp.where(jnp.arange(PROMPTS) == full, CACHE, drawn).astype(jnp.int32)


def block_scale(own_key, extent, pieces, smallest, top_value):
    gain, own = 1.0, jax.random.fold_in(own_key, 6)
    for dim, parts in pieces:
        draws = jnp.exp(jax.random.uniform(jax.random.fold_in(own, dim), (parts,), jnp.float32, smallest / len(pieces), top_value / len(pieces)))
        gain = gain * jnp.repeat(draws, extent[dim] // parts).reshape([-1 if axis == dim else 1 for axis in range(len(extent))])
    return gain


def shared_out(rng, own, number, rows, number_of, top, limit, skew):
    sequence = jax.random.permutation(rng, number_of)
    packed, common = portions_of(number_of, rows * top, limit, skew, True), portions_of(number_of, rows * top, limit, skew, False)
    places = jnp.arange(number_of)

    def named(sizes, turn):
        used = int((sizes > 0).sum())
        fixed = max(1, used // 4)
        passed = fixed + (places - fixed + turn * (used - fixed)) % max(1, number_of - fixed)
        return jnp.zeros((number_of,), jnp.int32).at[sequence[jnp.where(places < fixed, places, passed)]].set(jnp.asarray(sizes, jnp.int32))

    sizes = jnp.where(number % 4 == 0, named(packed, number // 4), named(common, number - number // 4 - 1))
    mixed = jax.random.permutation(jax.random.fold_in(own, 3), number_of)
    donor, taker = mixed[0:number_of // 2 * 2:2], mixed[1:number_of // 2 * 2:2]
    slack = jnp.minimum(sizes[donor] - 1, limit - sizes[taker]) // 2
    slack = jnp.where((donor == sequence[0]) | (taker == sequence[0]) | (sizes[taker] == 0), 0, jnp.maximum(slack, 0))
    passed = jax.random.randint(jax.random.fold_in(own, 4), (number_of // 2,), 0, 1 << 20) % (slack + 1)
    sizes = sizes.at[donor].add(-passed).at[taker].add(passed)
    labels = jnp.searchsorted(jnp.cumsum(sizes), jnp.arange(rows * top), side="right").astype(jnp.int32)
    listing = labels.reshape(top, rows).T
    listing = listing[jax.random.permutation(jax.random.fold_in(own, 1), rows)]
    turn = jax.random.randint(jax.random.fold_in(own, 2), (rows, 1), 0, top)
    return jnp.take_along_axis(listing, (jnp.arange(top)[None, :] + turn) % top, axis=1)


def portions_of(number_of, total, most, slope, full):
    weights = [(1 << 20) // math.isqrt(grade ** slope) + 1 for grade in range(1, number_of + 1)]
    largest = most if full else min(most, max(-(-total // number_of), total * weights[0] // sum(weights)))
    least = 1 if total - largest >= number_of - 1 else 0
    counts, surplus = [largest] + [least] * (number_of - 1), total - largest - least * (number_of - 1)
    while surplus > 0:
        movable = [i for i in range(1, number_of) if counts[i] < largest] or [i for i in range(1, number_of) if counts[i] < most]
        whole, left = sum([weights[i] for i in movable]), surplus
        for i in movable:
            extra = min(most - counts[i], max(1, left * weights[i] // whole), surplus)
            counts[i] = counts[i] + extra
            surplus = surplus - extra
    return np.array(counts)


def scatter_about(own_key, shape, scale, bound, shards=(), dtype=jnp.bfloat16):
    level = block_scale(own_key, shape, shards, -0.22, 0.18) if shards else 1.0
    values = jax.random.normal(own_key, shape, jnp.float32) * scale * level
    return jnp.minimum(jnp.maximum(values, -bound), bound).astype(dtype)


def setup_inputs(seed: int = 0) -> dict:
    seeds = jax.random.split(jax.random.key(seed), 12)
    queries = draw_queries(jax.random.fold_in(seeds[11], 71), 0)
    new_entries = scatter_about(seeds[1], (STRETCH, PROMPTS, KV_HEADS * 2 * HEAD_DIM), 1.5, 8.0, ((0, 16), (2, 8)))
    cached_entries = draw_cached_entries(jax.random.fold_in(seeds[11], 71), 0)
    cache_lengths = draw_cache_lengths(jax.random.fold_in(seeds[11], 71), 0)
    residual = scatter_about(seeds[4], (STRETCH, PROMPTS, D), 1.0, 6.0, ((0, 128),))
    out_weight = scatter_about(seeds[5], (Q_HEADS * HEAD_DIM, D), (Q_HEADS * HEAD_DIM) ** -0.5, 0.09375, ((0, 8), (1, 16)))
    norm_gain = jnp.clip(1.0 + 0.18 * jax.random.normal(seeds[6], (D,), jnp.float32), 0.1, 1.9)
    route_experts_keys = jax.random.split(jax.random.fold_in(seeds[7], 1), STRETCH * PROMPTS // TOK_DEV)
    route_experts_turns = jax.random.permutation(jax.random.fold_in(seeds[7], 3), STRETCH * PROMPTS // TOK_DEV)
    route_experts = jax.vmap(lambda own, number: shared_out(jax.random.fold_in(seeds[7], 2), own, number, TOK_DEV, EXPERTS, TOP, CAP, 2))(route_experts_keys, route_experts_turns).reshape((STRETCH, PROMPTS, TOP))
    route_weights = jnp.clip(0.1 + 0.5 * jax.random.uniform(seeds[8], (STRETCH, PROMPTS, TOP), jnp.float32) ** block_scale(seeds[8], (STRETCH, PROMPTS, TOP), ((0, 128),), -0.2, 0.2), 0.1, 0.6)
    inner_weight = scatter_about(seeds[9], (EXPERTS, D, 2 * FFW), D ** -0.5, 0.109375, ((0, 128),))
    outer_weight = scatter_about(seeds[10], (EXPERTS, FFW, D), FFW ** -0.5, 0.15625, ((0, 128),))
    return dict(queries=queries, new_entries=new_entries, cached_entries=cached_entries, cache_lengths=cache_lengths, residual=residual, out_weight=out_weight, norm_gain=norm_gain, route_experts=route_experts, route_weights=route_weights, inner_weight=inner_weight, outer_weight=outer_weight)


def reference(queries, new_entries, cached_entries, cache_lengths, residual, out_weight, norm_gain, route_experts, route_weights, inner_weight, outer_weight):
    group = Q_HEADS // KV_HEADS
    width = group * HEAD_DIM

    def attend_head(index):
        prompt = (index // KV_HEADS).astype(jnp.int32)
        head = (index % KV_HEADS).astype(jnp.int32)
        zero = jnp.int32(0)
        query_rows = lax.dynamic_slice(queries, (zero, prompt, head * width), (STRETCH, 1, width)).reshape(STRETCH, group, HEAD_DIM)
        cached = lax.dynamic_slice(cached_entries, (zero, prompt, head * 2 * HEAD_DIM), (CACHE, 1, 2 * HEAD_DIM)).reshape(CACHE, 2, HEAD_DIM)
        recent = lax.dynamic_slice(new_entries, (zero, prompt, head * 2 * HEAD_DIM), (STRETCH, 1, 2 * HEAD_DIM)).reshape(STRETCH, 2, HEAD_DIM)
        keys = jnp.concatenate([cached[:, 0], recent[:, 0]], axis=0).astype(jnp.float32)
        values = jnp.concatenate([cached[:, 1], recent[:, 1]], axis=0).astype(jnp.float32)
        scores = jnp.einsum('thd,jd->htj', query_rows.astype(jnp.float32), keys) * 0.125
        positions = jnp.arange(CACHE + STRETCH).astype(jnp.int32)
        rows = jnp.arange(STRETCH).astype(jnp.int32)
        length = cache_lengths[prompt]
        allowed = jnp.where(positions[None, :] < CACHE, positions[None, :] < length, positions[None, :] - CACHE <= rows[:, None])
        masked = jnp.where(allowed[None], scores, -jnp.inf)
        top = lax.optimization_barrier(jnp.max(masked, axis=-1, keepdims=True))
        expo = jnp.where(allowed[None], jnp.exp(scores - top), 0.0)
        total = lax.optimization_barrier(jnp.sum(expo, axis=-1, keepdims=True))
        probs = lax.optimization_barrier(expo.astype(jnp.bfloat16))
        mixed = jnp.einsum('htj,jd->htd', probs.astype(jnp.float32), values) / total
        return mixed.transpose(1, 0, 2).reshape(STRETCH, width).astype(jnp.bfloat16)
    attended = lax.map(attend_head, jnp.arange(PROMPTS * KV_HEADS).astype(jnp.int32))
    attended = attended.reshape(PROMPTS, KV_HEADS, STRETCH, width).transpose(2, 0, 1, 3).reshape(STRETCH * PROMPTS, Q_HEADS * HEAD_DIM)
    projected = jnp.dot(attended, out_weight, preferred_element_type=jnp.float32)
    hidden = residual.reshape(STRETCH * PROMPTS, D).astype(jnp.float32) + projected
    scale = lax.rsqrt(lax.optimization_barrier(jnp.mean(hidden * hidden, axis=-1, keepdims=True)) + 1e-05)
    normed = (hidden * scale * norm_gain[None, :]).astype(jnp.bfloat16)
    pairs = TOK_DEV * TOP
    chosen = route_experts.reshape(-1, pairs)
    blocks = chosen.shape[0]
    order = jnp.arange(pairs).astype(jnp.int32)
    earlier = (chosen[:, None, :] == chosen[:, :, None]) & (order[None, None, :] < order[None, :, None])
    slot = lax.optimization_barrier(jnp.sum(earlier.astype(jnp.int32), axis=-1)).astype(jnp.int32)
    place = (jnp.arange(blocks).astype(jnp.int32)[:, None] * CAP + slot).reshape(-1)
    expert_of = chosen.reshape(-1)
    source = normed[jnp.arange(blocks * pairs).astype(jnp.int32) // TOP]
    buffer = jnp.zeros((EXPERTS, blocks * CAP, D), jnp.bfloat16).at[expert_of, place].set(source)

    def expert_pass(items):
        batch, inner, outer = items
        lifted = jnp.dot(batch, inner, preferred_element_type=jnp.float32)
        gate = lifted[:, :FFW]
        upper = lifted[:, FFW:]
        active = ((upper + 1.0) * gate * jax.nn.sigmoid(1.702 * gate)).astype(jnp.bfloat16)
        return jnp.dot(active, outer, preferred_element_type=jnp.float32).astype(jnp.bfloat16)
    results = lax.map(expert_pass, (buffer, inner_weight, outer_weight))
    picked = results[expert_of, place].reshape(STRETCH * PROMPTS, TOP, D)
    mixture = lax.optimization_barrier(jnp.sum(route_weights.reshape(STRETCH * PROMPTS, TOP, 1) * picked.astype(jnp.float32), axis=1))
    return (hidden + mixture).reshape(STRETCH, PROMPTS, D).astype(jnp.bfloat16)
```

```python
import functools
import jax
import jax.numpy as jnp
from jax import lax
from jax.experimental import pallas as pl
from jax.experimental.pallas import tpu as pltpu
from jax.sharding import PartitionSpec as P

HEAD_DIM = 64
LANES = 128
NEGATIVE = -1e30


def attend_kernel(info_ref, q_ref, kv_ref, out_ref, rows_ref, cached_ref, recent_ref, score_ref, best_ref, accum_ref,
                  *, base, own, cached, tile, block):
    ctx_count = kv_ref.shape[0]
    tokens = q_ref.shape[0]
    recent = own * ctx_count
    per_block, per_recent = block // cached, block // own
    cached_blocks, recent_blocks = cached * ctx_count // block, recent // block
    length = info_ref[base + pl.program_id(0)]
    first = info_ref[info_ref.shape[0] - 1] * tokens
    pairs = q_ref.shape[1] // LANES
    low = lax.broadcasted_iota(jnp.int32, (tokens, LANES), 1) < HEAD_DIM
    for pair in range(pairs):
        both = q_ref[:, pair * LANES:(pair + 1) * LANES].astype(jnp.float32) * 0.125
        for odd in range(2):
            head = pltpu.roll(both, HEAD_DIM, 1) if odd else both
            rows_ref[pl.ds((2 * pair + odd) * tokens, tokens)] = jnp.where(low, head, 0.0).astype(jnp.bfloat16)
    def ones_beside(entries):
        lane = lax.broadcasted_iota(jnp.int32, entries.shape, 1)
        return jnp.where(lane < HEAD_DIM, 1.0, entries.astype(jnp.float32)).astype(jnp.bfloat16)

    @pl.loop(0, ctx_count)
    def _(c):
        cached_ref[pl.ds(c * cached, cached)] = ones_beside(kv_ref[c, :cached])
        recent_ref[pl.ds(c * own, own)] = ones_beside(kv_ref[c, cached:])

    whole = length // block
    rest = length - whole * block

    for start in range(0, rows_ref.shape[0], tile):
        rows = rows_ref[start:start + tile]

        def scores_of(keys):
            return lax.dot_general(rows, keys, (((1,), (1,)), ((), ())), preferred_element_type=jnp.float32)

        def cached_keys(b):
            return kv_ref[pl.ds(b * per_block, per_block), :cached].reshape(block, LANES)

        def keep(slot, scores):
            score_ref[slot] = scores
            best = best_ref[...]
            for part in range(0, block, LANES):
                best = jnp.maximum(best, scores[:, part:part + LANES])
            best_ref[...] = best

        best_ref[...] = jnp.full(best_ref.shape, NEGATIVE, jnp.float32)
        column = lax.broadcasted_iota(jnp.int32, (tile, block), 1)
        for b in range(recent_blocks):
            token = start + lax.broadcasted_iota(jnp.int32, (tile, block), 0)
            token = first + lax.rem(token, tokens)
            keys = kv_ref[b * per_recent:(b + 1) * per_recent, cached:].reshape(block, LANES)
            keep(cached_blocks + b, jnp.where(column + b * block <= token, scores_of(keys), NEGATIVE))

        @pl.loop(0, whole)
        def _(b):
            keep(b, scores_of(cached_keys(b)))

        @pl.when(rest > 0)
        def _():
            keep(whole, jnp.where(column < rest, scores_of(cached_keys(whole)), NEGATIVE))

        best_ref[...] = jnp.broadcast_to(jnp.max(best_ref[...], axis=1, keepdims=True), best_ref.shape)
        accum_ref[...] = jnp.zeros(accum_ref.shape, jnp.float32)

        def weigh(slot, entries):
            best = best_ref[...]
            probs = [
                jnp.exp(score_ref[slot, :, part:part + LANES] - best).astype(jnp.bfloat16)
                for part in range(0, block, LANES)
            ]
            accum_ref[...] += jnp.dot(jnp.concatenate(probs, axis=1), entries, preferred_element_type=jnp.float32)

        for b in range(recent_blocks):
            weigh(cached_blocks + b, recent_ref[b * block:(b + 1) * block])

        @pl.loop(0, (length + block - 1) // block)
        def _(b):
            weigh(b, cached_ref[pl.ds(pl.multiple_of(b * block, block), block)])

        accum = accum_ref[...]
        done = accum / pltpu.roll(accum, HEAD_DIM, 1)
        for at in range(start, start + tile, 2 * tokens):
            even = done[at - start:at - start + tokens]
            odd = done[at - start + tokens:at - start + 2 * tokens]
            pair = at // (2 * tokens)
            out_ref[:, pair * LANES:(pair + 1) * LANES] = jnp.where(low, pltpu.roll(even, HEAD_DIM, 1), odd).astype(jnp.bfloat16)


def attend(info, queries, entries, base, prompts, own, tile=512, block=1024):
    _, tokens, width = queries.shape
    _, ctx_count, held, _ = entries.shape
    cached = held - own
    rows = tokens * width // HEAD_DIM
    slots = ctx_count * held // block
    return pl.pallas_call(
        functools.partial(attend_kernel, base=base, own=own, cached=cached, tile=tile, block=block),
        out_shape=jax.ShapeDtypeStruct((prompts, tokens, width), jnp.bfloat16),
        grid=(prompts,),
        in_specs=[
            pl.BlockSpec(memory_space=pltpu.SMEM),
            pl.BlockSpec((None, tokens, width), lambda p: (base + p, 0, 0)),
            pl.BlockSpec((None, ctx_count, held, LANES), lambda p: (base + p, 0, 0, 0)),
        ],
        out_specs=pl.BlockSpec((None, tokens, width), lambda p: (p, 0, 0)),
        scratch_shapes=[
            pltpu.VMEM((rows, LANES), jnp.bfloat16),
            pltpu.VMEM((ctx_count * cached, LANES), jnp.bfloat16),
            pltpu.VMEM((ctx_count * own, LANES), jnp.bfloat16),
            pltpu.VMEM((slots, tile, block), jnp.float32),
            pltpu.VMEM((tile, LANES), jnp.float32),
            pltpu.VMEM((tile, LANES), jnp.float32),
        ],
        compiler_params=pltpu.CompilerParams(vmem_limit_bytes=46 * 2**20),
        cost_estimate=pl.CostEstimate(
            flops=8 * prompts * rows * ctx_count * held * HEAD_DIM,
            bytes_accessed=prompts * ctx_count * held * 2 * LANES,
            transcendentals=prompts * rows * ctx_count * held,
        ),
    )(info, queries, entries)


def project_kernel(attended_ref, weight_ref, out_ref, *, step):
    prompts, tokens, depth = attended_ref.shape
    members, _, width = out_ref.shape
    each = tokens // members
    attended = attended_ref[...].reshape(prompts * tokens, depth)
    for at in range(0, width, step):
        size = min(step, width - at)
        product = lax.dot_general(
            attended, weight_ref[at:at + size], (((1,), (1,)), ((), ())), preferred_element_type=jnp.float32
        ).astype(jnp.bfloat16)
        for prompt in range(prompts):
            out_ref[:, prompt * each:(prompt + 1) * each, at:at + size] = product[
                prompt * tokens:(prompt + 1) * tokens
            ].reshape(members, each, size)


def project(attended, weight, members, step=512):
    prompts, tokens, depth = attended.shape
    width = weight.shape[0]
    return pl.pallas_call(
        functools.partial(project_kernel, step=step),
        out_shape=jax.ShapeDtypeStruct((members, prompts * tokens // members, width), jnp.bfloat16),
        in_specs=[pl.BlockSpec(memory_space=pltpu.VMEM)] * 2,
        out_specs=pl.BlockSpec(memory_space=pltpu.VMEM),
        compiler_params=pltpu.CompilerParams(vmem_limit_bytes=24 * 2**20),
        cost_estimate=pl.CostEstimate(
            flops=2 * prompts * tokens * width * depth,
            bytes_accessed=2 * (weight.size + prompts * tokens * (depth + width)),
            transcendentals=0,
        ),
    )(attended, weight)


def pick_kernel(select_ref, rows_ref, out_ref, *, step):
    width = rows_ref.shape[1]
    for at in range(0, width, step):
        size = min(step, width - at)
        out_ref[:, at:at + size] = jnp.dot(
            select_ref[...], rows_ref[:, at:at + size], preferred_element_type=jnp.float32
        ).astype(jnp.bfloat16)


def pick(select, rows, step=512):
    return pl.pallas_call(
        functools.partial(pick_kernel, step=step),
        out_shape=jax.ShapeDtypeStruct((select.shape[0], rows.shape[1]), jnp.bfloat16),
        in_specs=[pl.BlockSpec(memory_space=pltpu.VMEM)] * 2,
        out_specs=pl.BlockSpec(memory_space=pltpu.VMEM),
        compiler_params=pltpu.CompilerParams(vmem_limit_bytes=24 * 2**20),
        cost_estimate=pl.CostEstimate(
            flops=2 * select.size * rows.shape[1], bytes_accessed=2 * select.shape[0] * rows.shape[1], transcendentals=0
        ),
    )(select, rows)


GROUP = 2


def exchange(value, axis):
    return lax.ppermute(value, axis, [(0, 1), (1, 0)])


ROWS = 64


def expert_kernel(rows_ref, inner_ref, outer_ref, out_ref, first_ref, second_ref, lifted_ref, active_ref, sems, *, step):
    count, width = rows_ref.shape
    half = outer_ref.shape[0]
    bounds = [(at, min(step, width - at)) for at in range(0, width, step)]
    lifts = [
        pltpu.make_async_copy(inner_ref.at[pl.ds(at, size)], first_ref.at[pl.ds(at, size)], sems.at[index])
        for index, (at, size) in enumerate(bounds)
    ]
    lowering = pltpu.make_async_copy(outer_ref, second_ref, sems.at[len(bounds)])
    for copy in lifts + [lowering]:
        copy.start()
    whole = width // step
    tail = width - whole * step

    def over_columns(body):
        @pl.loop(0, whole)
        def _(n):
            body(pl.ds(pl.multiple_of(n * step, step), step))

        if tail:
            body(pl.ds(whole * step, tail))

    for index, (at, size) in enumerate(bounds):
        lifts[index].wait()

        def lift(columns, at=at, size=size, index=index):
            part = jnp.dot(rows_ref[:, at:at + size], first_ref[at:at + size, columns], preferred_element_type=jnp.float32)
            if index:
                lifted_ref[:, columns] += part
            else:
                lifted_ref[:, columns] = part

        over_columns(lift)

    @pl.loop(0, count // ROWS)
    def _(r):
        some = pl.ds(pl.multiple_of(r * ROWS, ROWS), ROWS)
        gate = lifted_ref[some, :half]
        upper = lifted_ref[some, half:]
        sigmoid = 0.5 + 0.5 * jnp.tanh(0.851 * gate)
        active_ref[some] = ((upper + 1.0) * gate * sigmoid).astype(jnp.bfloat16)

    lowering.wait()

    def lower(columns):
        out_ref[:, columns] = jnp.dot(
            active_ref[...], second_ref[:, columns], preferred_element_type=jnp.float32
        ).astype(jnp.bfloat16)

    over_columns(lower)


def run_expert(rows, inner, outer, step=1536):
    count, width = rows.shape
    return pl.pallas_call(
        functools.partial(expert_kernel, step=step),
        out_shape=jax.ShapeDtypeStruct(rows.shape, jnp.bfloat16),
        in_specs=[
            pl.BlockSpec(memory_space=pltpu.VMEM),
            pl.BlockSpec(memory_space=pl.ANY),
            pl.BlockSpec(memory_space=pl.ANY),
        ],
        out_specs=pl.BlockSpec(memory_space=pltpu.VMEM),
        scratch_shapes=[
            pltpu.VMEM(inner.shape, jnp.bfloat16),
            pltpu.VMEM(outer.shape, jnp.bfloat16),
            pltpu.VMEM((count, inner.shape[1]), jnp.float32),
            pltpu.VMEM((count, outer.shape[0]), jnp.bfloat16),
            pltpu.SemaphoreType.DMA((-(-width // step) + 1,)),
        ],
        compiler_params=pltpu.CompilerParams(vmem_limit_bytes=50 * 2**20),
        cost_estimate=pl.CostEstimate(
            flops=2 * count * (inner.size + outer.size), bytes_accessed=2 * (inner.size + outer.size), transcendentals=0
        ),
    )(rows, inner, outer)


def slots_of(experts, core, wide_count, capacity, block):
    chosen = experts.reshape(-1)
    order = jnp.arange(chosen.shape[0])
    earlier = (chosen[None, :] == chosen[:, None]) & (order[None, :] < order[:, None])
    rank = jnp.sum(earlier.astype(jnp.int32), axis=1)
    chip = (chosen // (2 * wide_count)) * wide_count + chosen % wide_count
    here = (chosen // wide_count) % 2 == core
    return jnp.where(here, chip * (2 * capacity) + block * capacity + rank, -1).reshape(experts.shape)


def shards(
    queries,
    new_entries,
    cached_entries,
    cache_lengths,
    residual,
    out_weight,
    norm_gain,
    route_experts,
    route_weights,
    inner_weight,
    outer_weight,
):
    tokens, prompts, query_width = queries.shape
    owned, _, width = residual.shape
    members = lax.axis_size("wide")
    chips = lax.axis_size("zlo") * lax.axis_size("x") * members
    core = lax.axis_index("core")
    ctx = (lax.axis_index("zlo") * lax.axis_size("x") + lax.axis_index("x")) * 2 + core
    info = jnp.concatenate([cache_lengths, ctx.astype(jnp.int32)[None]])
    top = route_experts.shape[-1]

    experts = route_experts.transpose(1, 0, 2).reshape(-1, top)
    weights = route_weights.transpose(1, 0, 2).reshape(-1, top)
    here = experts.shape[0]
    capacity = 4
    slots = jnp.concatenate(
        [
            slots_of(experts, core, members, capacity, 0),
            slots_of(exchange(experts, "core"), core, members, capacity, 1),
        ]
    )
    shares = jnp.concatenate([weights, exchange(weights, "core")])
    slot_ids = jnp.arange(chips * 2 * capacity)
    match = slots[:, :, None] == slot_ids[None, None, :]
    select = jnp.any(match, axis=1).T.astype(jnp.bfloat16)

    entries = jnp.concatenate([cached_entries, new_entries], axis=0).transpose(1, 0, 2)
    held = lax.all_gather(entries, ("zlo", "x", "core"), axis=1, tiled=False)
    out_weight, held = lax.optimization_barrier((out_weight, held))
    full_weight = lax.all_gather(out_weight.T, ("zlo", "x", "core"), axis=0, tiled=True)
    stretch = queries.transpose(1, 0, 2)
    parts = []
    for base in range(0, prompts, GROUP):
        attended = attend(info, stretch, held, base, GROUP, tokens)
        product = project(attended, full_weight, members)
        parts.append(lax.all_to_all(product, "wide", split_axis=0, concat_axis=0, tiled=True))
    projected = jnp.concatenate([jnp.sum(part.astype(jnp.float32), axis=0) for part in parts])
    hidden = residual.transpose(1, 0, 2).reshape(-1, width).astype(jnp.float32) + projected

    scale = lax.rsqrt(jnp.mean(hidden * hidden, axis=-1, keepdims=True) + 1e-05)
    normed = (hidden * scale * norm_gain[None, :]).astype(jnp.bfloat16)
    both = jnp.concatenate([normed, exchange(normed, "core")])
    outgoing = pick(select, both)
    outgoing, shares, match = lax.optimization_barrier((outgoing, shares, match))
    share = jnp.sum(jnp.where(match, shares[:, :, None], 0.0), axis=1)
    share_high = share.astype(jnp.bfloat16)
    share_low = (share - share_high.astype(jnp.float32)).astype(jnp.bfloat16)

    def across(rows):
        swapped = lax.all_to_all(
            rows.reshape(chips, 2 * capacity, width), ("zlo", "x", "wide"), split_axis=0, concat_axis=0, tiled=True
        )
        return swapped.reshape(rows.shape)

    returned = across(run_expert(across(outgoing), inner_weight[0], outer_weight[0]))
    mixture = jnp.dot(share_high, returned, preferred_element_type=jnp.float32) + jnp.dot(
        share_low, returned, preferred_element_type=jnp.float32
    )
    others = exchange(mixture[here:].astype(jnp.bfloat16), "core").astype(jnp.float32)
    layer_out = (hidden + (mixture[:here] + others)).astype(jnp.bfloat16)
    return layer_out.reshape(prompts, owned, width).transpose(1, 0, 2)


def solution(mesh):
    ctx_count, wide_count = mesh.devices.shape
    split = jax.sharding.Mesh(
        mesh.devices.reshape(2, ctx_count // 4, 2, wide_count), ("zlo", "x", "core", "wide")
    )
    ctx = ("zlo", "x", "core")
    every = ctx + ("wide",)
    placed = (
        P(ctx, None, "wide"),
        P(ctx, None, "wide"),
        P(ctx, None, "wide"),
        P(),
        P(every, None, None),
        P("wide", ctx),
        P(),
        P(every, None, None),
        P(every, None, None),
        P(every, None, None),
        P(every, None, None),
    )
    return jax.shard_map(
        shards,
        mesh=split,
        in_specs=placed,
        out_specs=P(every, None, None),
        check_vma=False,
    )
```
